256 devices in a mesh: row: 16 (over y, z_lo, core), col: 16 (over x, z_hi).
Axes of the slice: x: 4, y: 4, z: 8 (z_hi: 4, z_lo: 2; z = z_hi * 2 + z_lo), core: 2. Of those that a mesh axis runs over, the one named last changes fastest.
Arguments:
- amplitudes: float32 [8192, 8192], P('row', 'col'), may hold values from -8 to 8, as said below
- factors: float32 [8192, 1536], P(('row', 'col')), may hold values from -1.5 to 1.5
- occ_map: int32 [8192], P(('row', 'col')), may hold values from 0 to 127
- vir_map: int32 [8192], P(('row', 'col')), may hold values from 0 to 1023
- occ_energy: float32 [128], replicated, may hold values from -2 to -0.3
- vir_energy: float32 [1024], replicated, may hold values from 0.2 to 3
Outputs:
- new_amplitudes: float32 [8192, 8192], P('row', 'col')
- density: float32 [8192, 1536], P('row', 'col')
The draws below stay inside these ranges and needn't reach their ends.
Inputs may be any that keep to these rules, and one draw needn't show every extreme that they name: amplitudes equals its transpose, up to float32 rounding.
All inputs are finite; a program needn't handle non-finite values.
Results may differ from the reference program's by a relative error of at most 0.00012.
Values sent between devices are 32-bit elements; how exact they have to be, the bound alone decides.
No kernel may reach another device: no remote copies, remote signals or barrier semaphores. Data moves between devices by JAX's collectives and lax.ppermute only.
A program may use at most 64 MiB of HBM per device.

```python
import jax
import jax.numpy as jnp
from jax import lax

NAUX = 1536
NOCC = 128
NVIR = 1024
NW = 8192
TR = 512
N_ROW = 16


def draw_amplitudes(key, part):
    base = jax.random.truncated_normal(key, -4.0, 4.0, (NW, NW), jnp.float32)
    sym = (base + base.T) * 0.5 ** 0.5 / NW ** 0.5
    return jnp.clip(sym, -8.0, 8.0)


def plant(result, stream_key, smallest, high):
    longest = result.shape.index(max(result.shape))
    spots = []
    for shift in (0, 1):
        where = [jax.random.randint(jax.random.fold_in(stream_key, axis), (), 0, length) for axis, length in enumerate(result.shape)]
        where[longest] = (where[longest] + shift) % result.shape[longest]
        spots.append(tuple(where))
    return result.at[spots[0]].set(smallest).at[spots[1]].set(high)


def block_levels(key, shape, pieces, low, high):
    loudness = 1.0
    for axis_at, parts in pieces:
        steps = jax.random.uniform(jax.random.fold_in(jax.random.fold_in(key, 6), axis_at), (parts,), jnp.float32, low / len(pieces), high / len(pieces))
        loudness = loudness * jnp.repeat(jnp.exp(steps), shape[axis_at] // parts).reshape((-1,) + (1,) * (len(shape) - 1 - axis_at))
    return loudness


def bell_draw(own_key, extent, scale, reach, split=(), dtype=jnp.bfloat16):
    level = block_levels(own_key, extent, split, -0.22, 0.18) if split else 1.0
    array = jax.random.normal(own_key, extent, jnp.float32) * scale * level
    return jnp.minimum(jnp.maximum(array, -reach), reach).astype(dtype)


def setup_inputs(seed: int = 0) -> dict:
    seeds = jax.random.split(jax.random.key(seed), 7)
    return {
        "amplitudes": draw_amplitudes(jax.random.fold_in(seeds[6], 71), 0),
        "factors": bell_draw(seeds[1], (NW, NAUX), 0.25, 1.5, ((0, 256),), jnp.float32),
        "occ_map": plant(jax.random.randint(seeds[2], (NW,), 0, NOCC), jax.random.fold_in(seeds[2], 1), 0, NOCC - 1).astype(jnp.int32),
        "vir_map": plant(jax.random.randint(seeds[3], (NW,), 0, NVIR), jax.random.fold_in(seeds[3], 1), 0, NVIR - 1).astype(jnp.int32),
        "occ_energy": jnp.clip(jax.random.uniform(seeds[4], (NOCC,), jnp.float32, -2.0, -0.3), -2.0, -0.3),
        "vir_energy": jnp.clip(jax.random.uniform(seeds[5], (NVIR,), jnp.float32, 0.2, 3.0), 0.2, 3.0),
    }


HIGHEST = lax.Precision.HIGHEST


def reference(amplitudes, factors, occ_map, vir_map, occ_energy, vir_energy):
    pair_energy = vir_energy[vir_map] - occ_energy[occ_map]
    mixed = jnp.dot(amplitudes, factors, precision=HIGHEST, preferred_element_type=jnp.float32)
    left_side = factors + mixed

    def one_block(block):
        left_rows, factor_rows, mixed_rows, energy_rows = block
        residual = jnp.dot(left_rows, factors.T, precision=HIGHEST, preferred_element_type=jnp.float32)
        residual = residual + jnp.dot(factor_rows, mixed.T, precision=HIGHEST, preferred_element_type=jnp.float32)
        new_amp = -residual / (energy_rows[:, None] + pair_energy[None, :])
        dens_rows = jnp.dot(new_amp, factors, precision=HIGHEST, preferred_element_type=jnp.float32)
        return new_amp, dens_rows

    new_amp, dens_rows = lax.map(one_block, (left_side.reshape(N_ROW, TR, NAUX), factors.reshape(N_ROW, TR, NAUX), mixed.reshape(N_ROW, TR, NAUX), pair_energy.reshape(N_ROW, TR)))
    return new_amp.reshape(NW, NW), dens_rows.reshape(NW, NAUX)
```

```python
import jax
import jax.numpy as jnp
from jax import lax
from jax.sharding import PartitionSpec as P

HIGH = lax.Precision.HIGH
CHUNKS = 2
LANES = 128


def look_up(table, index):
    hot = index[:, None] == jnp.arange(table.shape[0], dtype=jnp.int32)[None, :]
    return jnp.sum(jnp.where(hot, table[None, :], 0.0), axis=1)


def mul(a, b, da, db):
    return lax.dot_general(
        a, b, (((da,), (db,)), ((), ())), precision=HIGH, preferred_element_type=jnp.float32
    )


def per_device(amplitudes, factors, occ_map, vir_map, occ_energy, vir_energy):
    n = lax.axis_size("row")
    flip_pairs = [(i * n + j, j * n + i) for i in range(n) for j in range(n)]

    def flip(x):
        return lax.ppermute(x, ("row", "col"), flip_pairs)

    def sum_over_row(x):
        parts = lax.all_to_all(x, "row", 0, 0, tiled=True)
        return jnp.sum(parts.reshape(n, x.shape[0] // n, x.shape[1]), axis=0)

    energy = look_up(vir_energy, vir_map) - look_up(occ_energy, occ_map)
    energy = jnp.broadcast_to(energy[:, None], (energy.shape[0], LANES))
    naux = factors.shape[1]
    flipped = flip(jnp.concatenate([factors, energy], axis=1))
    step = naux // CHUNKS
    gathered = []
    for k in range(CHUNKS):
        piece = factors[:, k * step : (k + 1) * step]
        if gathered:
            piece, gathered[-1] = lax.optimization_barrier((piece, gathered[-1]))
        gathered.append(lax.all_gather(piece, "col", axis=0, tiled=True))
    halves = []
    row_energy = col_energy = None
    for k in range(CHUNKS):
        mixed = mul(amplitudes, gathered[k], 0, 0)
        if k == CHUNKS - 1:
            mixed, energy, flip_energy = lax.optimization_barrier(
                (mixed, energy, flipped[:, naux:])
            )
            row_energy = lax.all_gather(energy, "col", axis=0, tiled=True)
            col_energy = lax.all_gather(flip_energy, "row", axis=0, tiled=True)
        mine = sum_over_row(mixed) + 0.5 * flipped[:, k * step : (k + 1) * step]
        halves.append(lax.all_gather(mine, "row", axis=0, tiled=True))
    outgoing = sum(mul(x, f, 1, 1) for x, f in zip(halves, gathered))
    incoming = flip(outgoing)
    local = sum(mul(f, x, 1, 1) for x, f in zip(halves, gathered))
    new_amp = -(local + incoming) / (row_energy[:, :1] + col_energy[:, 0][None, :])
    dens = jnp.concatenate([mul(f, new_amp, 0, 0) for f in gathered], axis=0)
    density = flip(sum_over_row(dens)).T
    return (new_amp, density)


def solution(mesh):
    placed = (
        P("row", "col"),
        P(("row", "col"), None),
        P(("row", "col")),
        P(("row", "col")),
        P(),
        P(),
    )
    return jax.shard_map(
        per_device,
        mesh=mesh,
        in_specs=placed,
        out_specs=(P("row", "col"), P("row", "col")),
        check_vma=False,
    )
```

```python
import jax
import jax.numpy as jnp
from jax import lax
from jax.sharding import Mesh, PartitionSpec as P

HIGH = lax.Precision.HIGH
ALL = ("pair", "core", "col")
CORES = 2


def look_up(table, index):
    hot = index[:, None] == jnp.arange(table.shape[0], dtype=jnp.int32)[None, :]
    return jnp.sum(jnp.where(hot, table[None, :], 0.0), axis=1)


def mul(a, b, da, db):
    return lax.dot_general(
        a, b, (((da,), (db,)), ((), ())), precision=HIGH, preferred_element_type=jnp.float32
    )


def per_device(amplitudes, factors, occ_map, vir_map, occ_energy, vir_energy):
    pairs, n = lax.axis_size("pair"), lax.axis_size("col")
    core = lax.axis_index("core")
    rows, naux = factors.shape
    half = naux // CORES
    flip_pairs = [(i * n + j, j * n + i) for i in range(n) for j in range(n)]
    swap_pairs = [(0, 1), (1, 0)]
    home_pairs = [
        ((p * CORES + c) * n + j, j * n + c * pairs + p)
        for p in range(pairs)
        for c in range(CORES)
        for j in range(n)
    ]

    def flip(x):
        return lax.ppermute(x, ALL, flip_pairs)

    def swap(x):
        return lax.ppermute(x, "core", swap_pairs)

    def both(own, other, axis):
        first = jnp.where(core == 0, own, other)
        second = jnp.where(core == 0, other, own)
        return jnp.stack([first, second], axis=axis)

    def split_factors(x):
        own = lax.dynamic_slice_in_dim(x, core * half, half, axis=1)
        away = lax.dynamic_slice_in_dim(x, (1 - core) * half, half, axis=1)
        return both(own, swap(away), 0).reshape(CORES * x.shape[0], half)

    def spread(x, axis, copies):
        x = jnp.broadcast_to(x[None], (copies, *x.shape))
        x = x.reshape(copies * x.shape[1], x.shape[2])
        return lax.all_to_all(x, axis, 0, 0, tiled=True)

    def sum_over_pairs(x):
        parts = lax.all_to_all(x, "pair", 0, 0, tiled=True)
        return jnp.sum(parts.reshape(pairs, x.shape[0] // pairs, x.shape[1]), axis=0)

    row_factor = lax.all_gather(split_factors(factors), "col", axis=0, tiled=True)

    energy = look_up(vir_energy, vir_map) - look_up(occ_energy, occ_map)
    energy = jnp.broadcast_to(jnp.pad(energy, (0, 128 - rows))[None], (8, 128))
    row_energy = spread(energy, "col", n).reshape(n, 8, 128)[:, 0, :rows].reshape(n * rows)
    col_energy = spread(flip(energy), ("pair", "core"), n)
    col_energy = col_energy.reshape(n, 8, 128)[:, 0, :rows].reshape(n * rows)
    flipped = split_factors(flip(factors))

    tile = amplitudes.shape[0]
    width = amplitudes.shape[1]
    own_amp = amplitudes.reshape(n, rows, width)
    amp = both(own_amp, swap(amplitudes).reshape(n, rows, width), 1)
    amp = amp.reshape(CORES * tile, width)
    amp, row_energy, col_energy = lax.optimization_barrier((amp, row_energy, col_energy))

    mixed = sum_over_pairs(mul(amp, row_factor, 0, 0))
    col_x = spread(mixed + 0.5 * flipped, "pair", pairs)

    by_core = row_factor.reshape(n, CORES, rows, half)
    own_factor = lax.dynamic_index_in_dim(by_core, core, 1, keepdims=False).reshape(tile, half)
    far_factor = lax.dynamic_index_in_dim(by_core, 1 - core, 1, keepdims=False).reshape(tile, half)
    outgoing = swap(mul(col_x, far_factor, 1, 1)) + mul(col_x, own_factor, 1, 1)
    residual = flip(outgoing) + outgoing.T
    new_amp = -residual / (row_energy[:, None] + col_energy[None, :])

    dens = mul(far_factor, swap(new_amp), 0, 0) + mul(own_factor, new_amp, 0, 0)
    density = lax.ppermute(sum_over_pairs(dens), ALL, home_pairs).T
    return (new_amp, density)


def solution(mesh):
    shape = mesh.devices.shape
    grid = Mesh(mesh.devices.reshape(shape[0] // CORES, CORES, shape[1]), ALL)
    rows = ("pair", "core")
    placed = (
        P(rows, "col"),
        P(ALL, None),
        P(ALL),
        P(ALL),
        P(),
        P(),
    )
    return jax.shard_map(
        per_device,
        mesh=grid,
        in_specs=placed,
        out_specs=(P(rows, "col"), P(rows, "col")),
        check_vma=False,
    )
```

```python
import jax
import jax.numpy as jnp
from jax import lax
from jax.sharding import Mesh, PartitionSpec as P

HIGH = lax.Precision.HIGH
COL = ("x", "deep")
ALL = ("pair", "core", *COL)
CORES = 2
RING = 4


def look_up(table, index):
    hot = index[:, None] == jnp.arange(table.shape[0], dtype=jnp.int32)[None, :]
    return jnp.sum(jnp.where(hot, table[None, :], 0.0), axis=1)


def mul(a, b, da, db):
    return lax.dot_general(
        a, b, (((da,), (db,)), ((), ())), precision=HIGH, preferred_element_type=jnp.float32
    )


def per_device(amplitudes, factors, occ_map, vir_map, occ_energy, vir_energy):
    pairs, n = lax.axis_size("pair"), lax.axis_size(COL)
    core, ring_at = lax.axis_index("core"), lax.axis_index("x")
    rows, naux = factors.shape
    half = naux // CORES
    early = half // 2
    flip_pairs = [(i * n + j, j * n + i) for i in range(n) for j in range(n)]
    swap_pairs = [(0, 1), (1, 0)]
    home_pairs = [
        ((p * CORES + c) * n + j, j * n + c * pairs + p)
        for p in range(pairs)
        for c in range(CORES)
        for j in range(n)
    ]

    def flip(x):
        return lax.ppermute(x, ALL, flip_pairs)

    def swap(x):
        return lax.ppermute(x, "core", swap_pairs)

    def both(own, other, axis):
        first = jnp.where(core == 0, own, other)
        second = jnp.where(core == 0, other, own)
        return jnp.stack([first, second], axis=axis)

    def split_factors(x):
        own = lax.dynamic_slice_in_dim(x, core * half, half, axis=1)
        away = lax.dynamic_slice_in_dim(x, (1 - core) * half, half, axis=1)
        return both(own, swap(away), 0).reshape(CORES * x.shape[0], half)

    def spread(x, axis, copies):
        x = jnp.broadcast_to(x[None], (copies, *x.shape))
        x = x.reshape(copies * x.shape[1], x.shape[2])
        return lax.all_to_all(x, axis, 0, 0, tiled=True)

    def sum_over_pairs(x):
        parts = lax.all_to_all(x, "pair", 0, 0, tiled=True)
        return jnp.sum(parts.reshape(pairs, x.shape[0] // pairs, x.shape[1]), axis=0)

    def shift(x, by):
        return lax.ppermute(x, "x", [(k, (k + by) % RING) for k in range(RING)])

    def ring_gather(x):
        left, right = shift(x, 1), shift(x, -1)
        mid = x.shape[0] // 2
        across = jnp.concatenate([shift(right[:mid], -1), shift(left[mid:], 1)], axis=0)
        out = jnp.zeros((RING, *x.shape), x.dtype)
        for by, block in ((0, x), (3, left), (1, right), (2, across)):
            at = lax.rem(ring_at + by, RING)
            out = lax.dynamic_update_slice(out, block[None], (at, 0, 0))
        return out.reshape(RING * x.shape[0], x.shape[1])

    shard = split_factors(factors)
    late_factor = lax.all_gather(shard[:, early:], COL, axis=0, tiled=True)
    near = spread(shard[:, :early], "deep", n // RING)

    energy = look_up(vir_energy, vir_map) - look_up(occ_energy, occ_map)
    energy = jnp.broadcast_to(jnp.pad(energy, (0, 128 - rows))[None], (8, 128))
    energy, near = lax.optimization_barrier((energy, near))
    row_energy = spread(energy, COL, n).reshape(n, 8, 128)[:, 0, :rows].reshape(1, n * rows)
    col_energy = flip(jnp.broadcast_to(row_energy, (8, n * rows)))[:1]
    flipped = split_factors(flip(factors))
    row_factor = [ring_gather(near), late_factor]

    tile = amplitudes.shape[0]
    width = amplitudes.shape[1]
    own_amp = amplitudes.reshape(n, rows, width)
    amp = both(own_amp, swap(amplitudes).reshape(n, rows, width), 1)
    amp = amp.reshape(CORES * tile, width)
    amp, row_energy, col_energy, flipped = lax.optimization_barrier(
        (amp, row_energy, col_energy, flipped)
    )

    outgoing = []
    own, far, sums = [], [], []
    for k, factor in enumerate(row_factor):
        if k:
            factor, last = lax.optimization_barrier((factor, sums[-1][0]))
            sums[-1] = (last, sums[-1][1])
        mixed = sum_over_pairs(mul(amp, factor, 0, 0))
        bare = flipped[:, :early] if k == 0 else flipped[:, early:]
        col_x = mixed + 0.5 * bare
        sums.append((col_x, factor))
    for k, (col_x, factor) in enumerate(sums):
        col_x = spread(col_x, "pair", pairs)
        by_core = factor.reshape(n, CORES, rows, factor.shape[1])
        for c, kept in ((core, own), (1 - core, far)):
            part = lax.dynamic_index_in_dim(by_core, c, 1, keepdims=False)
            kept.append(part.reshape(tile, factor.shape[1]))
        outgoing.append((mul(col_x, far[k], 1, 1), mul(col_x, own[k], 1, 1)))
    outgoing = swap(outgoing[0][0] + outgoing[1][0]) + (outgoing[0][1] + outgoing[1][1])
    residual = flip(outgoing) + outgoing.T
    new_amp = -residual / (row_energy.T + col_energy)

    far_amp = swap(new_amp)
    dens = jnp.concatenate(
        [mul(o, new_amp, 0, 0) + mul(f, far_amp, 0, 0) for o, f in zip(own, far)], axis=0
    )
    density = lax.ppermute(sum_over_pairs(dens), ALL, home_pairs).T
    return (new_amp, density)


def solution(mesh):
    shape = mesh.devices.shape
    grid = Mesh(mesh.devices.reshape(shape[0] // CORES, CORES, RING, shape[1] // RING), ALL)
    rows = ("pair", "core")
    placed = (
        P(rows, COL),
        P(ALL, None),
        P(ALL),
        P(ALL),
        P(),
        P(),
    )
    return jax.shard_map(
        per_device,
        mesh=grid,
        in_specs=placed,
        out_specs=(P(rows, COL), P(rows, COL)),
        check_vma=False,
    )
```

```python
import jax
import jax.numpy as jnp
from jax import lax
from jax.sharding import Mesh, PartitionSpec as P

HIGH = lax.Precision.HIGH
COL = "col"
ALL = ("pair", "core", COL)
CORES = 2


def look_up(table, index):
    hot = index[:, None] == jnp.arange(table.shape[0], dtype=jnp.int32)[None, :]
    return jnp.sum(jnp.where(hot, table[None, :], 0.0), axis=1)


def mul(a, b, da, db):
    return lax.dot_general(
        a, b, (((da,), (db,)), ((), ())), precision=HIGH, preferred_element_type=jnp.float32
    )


def per_device(amplitudes, factors, occ_map, vir_map, occ_energy, vir_energy):
    pairs, n = lax.axis_size("pair"), lax.axis_size(COL)
    core = lax.axis_index("core")
    rows, naux = factors.shape
    half = naux // CORES
    flip_pairs = [(i * n + j, j * n + i) for i in range(n) for j in range(n)]
    swap_pairs = [(0, 1), (1, 0)]
    home_pairs = [
        ((p * CORES + c) * n + j, j * n + c * pairs + p)
        for p in range(pairs)
        for c in range(CORES)
        for j in range(n)
    ]

    def flip(x):
        return lax.ppermute(x, ALL, flip_pairs)

    def swap(x):
        return lax.ppermute(x, "core", swap_pairs)

    def both(own, other, axis):
        first = jnp.where(core == 0, own, other)
        second = jnp.where(core == 0, other, own)
        return jnp.stack([first, second], axis=axis)

    def split_factors(x):
        own = lax.dynamic_slice_in_dim(x, core * half, half, axis=1)
        away = lax.dynamic_slice_in_dim(x, (1 - core) * half, half, axis=1)
        return both(own, swap(away), 0).reshape(CORES * x.shape[0], half)

    def spread(x, axis, copies):
        x = jnp.broadcast_to(x[None], (copies, *x.shape))
        x = x.reshape(copies * x.shape[1], x.shape[2])
        return lax.all_to_all(x, axis, 0, 0, tiled=True)

    def sum_over_pairs(x):
        parts = lax.all_to_all(x, "pair", 0, 0, tiled=True)
        return jnp.sum(parts.reshape(pairs, x.shape[0] // pairs, x.shape[1]), axis=0)

    shard = split_factors(factors)
    row_factor = lax.all_gather(shard, COL, axis=0, tiled=True)
    energy = look_up(vir_energy, vir_map) - look_up(occ_energy, occ_map)
    energy = jnp.broadcast_to(jnp.pad(energy, (0, 128 - rows))[None], (8, 128))
    row_energy = spread(energy, COL, n).reshape(n, 8, 128)[:, 0, :rows].reshape(1, n * rows)
    col_energy = flip(jnp.broadcast_to(row_energy, (8, n * rows)))[:1]
    flipped = split_factors(flip(factors))

    tile = amplitudes.shape[0]
    width = amplitudes.shape[1]
    own_amp = amplitudes.reshape(n, rows, width)
    amp = both(own_amp, swap(amplitudes).reshape(n, rows, width), 1)
    amp = amp.reshape(CORES * tile, width)
    amp, row_energy, col_energy, flipped = lax.optimization_barrier(
        (amp, row_energy, col_energy, flipped)
    )

    mixed = mul(amp, row_factor, 0, 0)
    col_x = spread(sum_over_pairs(mixed) + 0.5 * flipped, "pair", pairs)
    by_core = row_factor.reshape(n, CORES, rows, half)
    own, far = [
        lax.dynamic_index_in_dim(by_core, c, 1, keepdims=False).reshape(tile, half)
        for c in (core, 1 - core)
    ]

    mid = width // 2
    halves = [slice(k * mid, (k + 1) * mid) for k in range(2)]
    local, received = [], []
    for cols in halves:
        sent = swap(mul(col_x, far[cols], 1, 1)) + mul(col_x, own[cols], 1, 1)
        local.append(sent.T)
        if received:
            sent, received[0] = lax.optimization_barrier((sent, received[0]))
        received.append(flip(sent))
    local = jnp.concatenate(local, axis=0)
    amps, dens = [], []
    for k, cols in enumerate(halves):
        if k:
            received[k], _ = lax.optimization_barrier((received[k], part))
        new = -(received[k] + local[:, cols]) / (row_energy.T + col_energy[:, cols])
        part = sum_over_pairs(mul(far, swap(new), 0, 0) + mul(own, new, 0, 0))
        dens.append(lax.ppermute(part, ALL, home_pairs).T)
        amps.append(new)
    return (jnp.concatenate(amps, axis=1), jnp.concatenate(dens, axis=0))


def solution(mesh):
    shape = mesh.devices.shape
    grid = Mesh(mesh.devices.reshape(shape[0] // CORES, CORES, shape[1]), ALL)
    rows = ("pair", "core")
    placed = (
        P(rows, COL),
        P(ALL, None),
        P(ALL),
        P(ALL),
        P(),
        P(),
    )
    return jax.shard_map(
        per_device,
        mesh=grid,
        in_specs=placed,
        out_specs=(P(rows, COL), P(rows, COL)),
        check_vma=False,
    )
```

```python
import jax
import jax.numpy as jnp
from jax import lax
from jax.sharding import Mesh, PartitionSpec as P

HIGH = lax.Precision.HIGH
COL = ("x", "deep")
ALL = ("pair", "core", *COL)
CORES = 2
RING = 4


def look_up(table, index):
    hot = index[:, None] == jnp.arange(table.shape[0], dtype=jnp.int32)[None, :]
    return jnp.sum(jnp.where(hot, table[None, :], 0.0), axis=1)


def mul(a, b, da, db):
    return lax.dot_general(
        a, b, (((da,), (db,)), ((), ())), precision=HIGH, preferred_element_type=jnp.float32
    )


def per_device(amplitudes, factors, occ_map, vir_map, occ_energy, vir_energy):
    pairs, n = lax.axis_size("pair"), lax.axis_size(COL)
    core = lax.axis_index("core")
    rows, naux = factors.shape
    half = naux // CORES
    early = half // 2
    ring = lax.axis_size("x")
    flip_pairs = [(i * n + j, j * n + i) for i in range(n) for j in range(n)]
    swap_pairs = [(0, 1), (1, 0)]
    home_pairs = [
        ((p * CORES + c) * n + j, j * n + c * pairs + p)
        for p in range(pairs)
        for c in range(CORES)
        for j in range(n)
    ]

    def flip(x):
        return lax.ppermute(x, ALL, flip_pairs)

    def swap(x):
        return lax.ppermute(x, "core", swap_pairs)

    def both(own, other, axis):
        first = jnp.where(core == 0, own, other)
        second = jnp.where(core == 0, other, own)
        return jnp.stack([first, second], axis=axis)

    def split_factors(x):
        own = lax.dynamic_slice_in_dim(x, core * half, half, axis=1)
        away = lax.dynamic_slice_in_dim(x, (1 - core) * half, half, axis=1)
        return both(own, swap(away), 0).reshape(CORES * x.shape[0], half)

    def spread(x, axis, copies):
        x = jnp.broadcast_to(x[None], (copies, *x.shape))
        x = x.reshape(copies * x.shape[1], x.shape[2])
        return lax.all_to_all(x, axis, 0, 0, tiled=True)

    def sum_over_pairs(x):
        parts = lax.all_to_all(x, "pair", 0, 0, tiled=True)
        return jnp.sum(parts.reshape(pairs, x.shape[0] // pairs, x.shape[1]), axis=0)

    shard = split_factors(factors)
    row_factor = lax.all_gather(shard, COL, axis=0, tiled=True)
    energy = look_up(vir_energy, vir_map) - look_up(occ_energy, occ_map)
    energy = jnp.broadcast_to(jnp.pad(energy, (0, 128 - rows))[None], (8, 128))
    row_energy = spread(energy, COL, n).reshape(n, 8, 128)[:, 0, :rows].reshape(1, n * rows)
    col_energy = flip(jnp.broadcast_to(row_energy, (8, n * rows)))[:1]
    flipped = split_factors(flip(factors))

    tile = amplitudes.shape[0]
    width = amplitudes.shape[1]
    own_amp = amplitudes.reshape(n, rows, width)
    amp = both(own_amp, swap(amplitudes).reshape(n, rows, width), 1)
    amp = amp.reshape(CORES * tile, width)
    amp, row_energy, col_energy, flipped = lax.optimization_barrier(
        (amp, row_energy, col_energy, flipped)
    )

    mixed = mul(amp, row_factor, 0, 0)
    col_x = spread(sum_over_pairs(mixed) + 0.5 * flipped, "pair", pairs)
    by_core = row_factor.reshape(n, CORES, rows, half)
    own, far = [
        lax.dynamic_index_in_dim(by_core, c, 1, keepdims=False).reshape(tile, half)
        for c in (core, 1 - core)
    ]

    away = swap(mul(col_x, far, 1, 1))
    outgoing = away + mul(col_x, own, 1, 1)
    residual = flip(outgoing) + outgoing.T
    new_amp = -residual / (row_energy.T + col_energy)
    dens = mul(far, swap(new_amp), 0, 0) + mul(own, new_amp, 0, 0)
    density = lax.ppermute(sum_over_pairs(dens), ALL, home_pairs).T
    return (new_amp, density)


def solution(mesh):
    shape = mesh.devices.shape
    grid = Mesh(mesh.devices.reshape(shape[0] // CORES, CORES, RING, shape[1] // RING), ALL)
    rows = ("pair", "core")
    placed = (
        P(rows, COL),
        P(ALL, None),
        P(ALL),
        P(ALL),
        P(),
        P(),
    )
    return jax.shard_map(
        per_device,
        mesh=grid,
        in_specs=placed,
        out_specs=(P(rows, COL), P(rows, COL)),
        check_vma=False,
    )
```

```python
import jax
import jax.numpy as jnp
from jax import lax
from jax.sharding import Mesh, PartitionSpec as P

HIGH = lax.Precision.HIGH
COL = ("x", "deep")
ALL = ("pair", "core", *COL)
CORES = 2
RING = 4


def look_up(table, index):
    hot = index[:, None] == jnp.arange(table.shape[0], dtype=jnp.int32)[None, :]
    return jnp.sum(jnp.where(hot, table[None, :], 0.0), axis=1)


def mul(a, b, da, db):
    return lax.dot_general(
        a, b, (((da,), (db,)), ((), ())), precision=HIGH, preferred_element_type=jnp.float32
    )


def per_device(amplitudes, factors, occ_map, vir_map, occ_energy, vir_energy):
    pairs, n = lax.axis_size("pair"), lax.axis_size(COL)
    core = lax.axis_index("core")
    rows, naux = factors.shape
    half = naux // CORES
    ring = lax.axis_size("x")
    flip_pairs = [(i * n + j, j * n + i) for i in range(n) for j in range(n)]
    swap_pairs = [(0, 1), (1, 0)]
    home_pairs = [
        ((p * CORES + c) * n + j, j * n + c * pairs + p)
        for p in range(pairs)
        for c in range(CORES)
        for j in range(n)
    ]

    def flip(x):
        return lax.ppermute(x, ALL, flip_pairs)

    def swap(x):
        return lax.ppermute(x, "core", swap_pairs)

    def both(own, other, axis):
        first = jnp.where(core == 0, own, other)
        second = jnp.where(core == 0, other, own)
        return jnp.stack([first, second], axis=axis)

    def split_factors(x):
        own = lax.dynamic_slice_in_dim(x, core * half, half, axis=1)
        away = lax.dynamic_slice_in_dim(x, (1 - core) * half, half, axis=1)
        return both(own, swap(away), 0).reshape(CORES * x.shape[0], half)

    def spread(x, axis, copies):
        x = jnp.broadcast_to(x[None], (copies, *x.shape))
        x = x.reshape(copies * x.shape[1], x.shape[2])
        return lax.all_to_all(x, axis, 0, 0, tiled=True)

    def sum_over_pairs(x):
        parts = lax.all_to_all(x, "pair", 0, 0, tiled=True)
        return jnp.sum(parts.reshape(pairs, x.shape[0] // pairs, x.shape[1]), axis=0)

    def shift(x, by):
        return lax.ppermute(x, "x", [(k, (k + by) % ring) for k in range(ring)])

    def ring_gather(x):
        left, right = shift(x, 1), shift(x, -1)
        part = x.shape[0] // 2
        across = [shift(right[:part], -1), shift(left[part:], 1)]
        at = lax.axis_index("x")
        out = jnp.zeros((ring, *x.shape), x.dtype)
        for by, row, block in (
            (0, 0, x), (3, 0, left), (1, 0, right), (2, 0, across[0]), (2, part, across[1])
        ):
            where = (lax.rem(at + by, ring), row, 0)
            out = lax.dynamic_update_slice(out, block[None], where)
        return out.reshape(ring * x.shape[0], x.shape[1])

    near = lax.all_gather(split_factors(factors), "deep", axis=0, tiled=True)
    row_factor = ring_gather(near)
    energy = look_up(vir_energy, vir_map) - look_up(occ_energy, occ_map)
    energy = jnp.broadcast_to(jnp.pad(energy, (0, 128 - rows))[None], (8, 128))
    row_energy = spread(energy, COL, n).reshape(n, 8, 128)[:, 0, :rows].reshape(1, n * rows)
    col_energy = flip(jnp.broadcast_to(row_energy, (8, n * rows)))[:1]

    tile = amplitudes.shape[0]
    width = amplitudes.shape[1]
    on_diagonal = lax.axis_index(("pair", "core")) == lax.axis_index(COL)
    half_unit = jnp.where(on_diagonal, 0.5, 0.0) * jnp.eye(tile, width, dtype=jnp.float32)
    own_amp = amplitudes + half_unit
    far_amp = swap(own_amp).reshape(n, rows, width)
    amp = both(own_amp.reshape(n, rows, width), far_amp, 1).reshape(CORES * tile, width)

    col_x = spread(sum_over_pairs(mul(amp, row_factor, 0, 0)), "pair", pairs)
    by_core = row_factor.reshape(n, CORES, rows, half)
    own, far = [
        lax.dynamic_index_in_dim(by_core, c, 1, keepdims=False).reshape(tile, half)
        for c in (core, 1 - core)
    ]

    away = swap(mul(col_x, far, 1, 1))
    outgoing = away + mul(col_x, own, 1, 1)
    residual = flip(outgoing) + outgoing.T
    new_amp = -residual / (row_energy.T + col_energy)
    dens = mul(far, swap(new_amp), 0, 0) + mul(own, new_amp, 0, 0)
    density = lax.ppermute(sum_over_pairs(dens), ALL, home_pairs).T
    return (new_amp, density)


def solution(mesh):
    shape = mesh.devices.shape
    grid = Mesh(mesh.devices.reshape(shape[0] // CORES, CORES, RING, shape[1] // RING), ALL)
    rows = ("pair", "core")
    placed = (
        P(rows, COL),
        P(ALL, None),
        P(ALL),
        P(ALL),
        P(),
        P(),
    )
    return jax.shard_map(
        per_device,
        mesh=grid,
        in_specs=placed,
        out_specs=(P(rows, COL), P(rows, COL)),
        check_vma=False,
    )
```

```python
import jax
import jax.numpy as jnp
from jax import lax
from jax.sharding import Mesh, PartitionSpec as P

HIGH = lax.Precision.HIGH
COL = ("x", "deep")
ALL = ("pair", "core", *COL)
CORES = 2
RING = 4


def look_up(table, index):
    hot = index[:, None] == jnp.arange(table.shape[0], dtype=jnp.int32)[None, :]
    return jnp.sum(jnp.where(hot, table[None, :], 0.0), axis=1)


def mul(a, b, da, db):
    return lax.dot_general(
        a, b, (((da,), (db,)), ((), ())), precision=HIGH, preferred_element_type=jnp.float32
    )


def per_device(amplitudes, factors, occ_map, vir_map, occ_energy, vir_energy):
    pairs, n = lax.axis_size("pair"), lax.axis_size(COL)
    core = lax.axis_index("core")
    rows, naux = factors.shape
    half = naux // CORES
    ring = lax.axis_size("x")
    flip_pairs = [(i * n + j, j * n + i) for i in range(n) for j in range(n)]
    swap_pairs = [(0, 1), (1, 0)]
    home_pairs = [
        ((p * CORES + c) * n + j, j * n + c * pairs + p)
        for p in range(pairs)
        for c in range(CORES)
        for j in range(n)
    ]

    def flip(x):
        return lax.ppermute(x, ALL, flip_pairs)

    def swap(x):
        return lax.ppermute(x, "core", swap_pairs)

    def both(own, other, axis):
        first = jnp.where(core == 0, own, other)
        second = jnp.where(core == 0, other, own)
        return jnp.stack([first, second], axis=axis)

    def split_factors(x):
        own = lax.dynamic_slice_in_dim(x, core * half, half, axis=1)
        away = lax.dynamic_slice_in_dim(x, (1 - core) * half, half, axis=1)
        return both(own, swap(away), 0).reshape(CORES * x.shape[0], half)

    def spread(x, axis, copies):
        x = jnp.broadcast_to(x[None], (copies, *x.shape))
        x = x.reshape(copies * x.shape[1], x.shape[2])
        return lax.all_to_all(x, axis, 0, 0, tiled=True)

    def sum_over_pairs(x):
        parts = lax.all_to_all(x, "pair", 0, 0, tiled=True)
        return jnp.sum(parts.reshape(pairs, x.shape[0] // pairs, x.shape[1]), axis=0)

    def shift(x, by):
        return lax.ppermute(x, "x", [(k, (k + by) % ring) for k in range(ring)])

    def ring_gather(x):
        left, right = shift(x, 1), shift(x, -1)
        part = x.shape[0] // 2
        across = [shift(right[:part], -1), shift(left[part:], 1)]
        at = lax.axis_index("x")
        out = jnp.zeros((ring, *x.shape), x.dtype)
        for by, row, block in (
            (0, 0, x), (3, 0, left), (1, 0, right), (2, 0, across[0]), (2, part, across[1])
        ):
            where = (lax.rem(at + by, ring), row, 0)
            out = lax.dynamic_update_slice(out, block[None], where)
        return out.reshape(ring * x.shape[0], x.shape[1])

    near = lax.all_gather(split_factors(factors), "deep", axis=0, tiled=True)
    row_factor = ring_gather(near)
    energy = look_up(vir_energy, vir_map) - look_up(occ_energy, occ_map)
    energy = jnp.broadcast_to(jnp.pad(energy, (0, 128 - rows))[None], (8, 128))

    tile = amplitudes.shape[0]
    width = amplitudes.shape[1]
    on_diagonal = lax.axis_index(("pair", "core")) == lax.axis_index(COL)
    half_unit = jnp.where(on_diagonal, 0.5, 0.0) * jnp.eye(tile, width, dtype=jnp.float32)
    own_amp = amplitudes + half_unit
    far_amp = swap(own_amp).reshape(n, rows, width)
    amp = both(own_amp.reshape(n, rows, width), far_amp, 1).reshape(CORES * tile, width)
    shard = sum_over_pairs(mul(amp, row_factor, 0, 0))
    energy, _ = lax.optimization_barrier((energy, shard))
    row_energy = spread(energy, COL, n).reshape(n, 8, 128)[:, 0, :rows].reshape(1, n * rows)
    col_x, row_energy = lax.optimization_barrier((spread(shard, "pair", pairs), row_energy))
    col_energy = flip(jnp.broadcast_to(row_energy, (8, n * rows)))[:1]
    by_core = row_factor.reshape(n, CORES, rows, half)
    own, far = [
        lax.dynamic_index_in_dim(by_core, c, 1, keepdims=False).reshape(tile, half)
        for c in (core, 1 - core)
    ]

    away = swap(mul(col_x, far, 1, 1))
    outgoing = away + lax.optimization_barrier(mul(col_x, own, 1, 1))
    mid = tile // 2
    direct = flip(outgoing[:mid])
    block = n // ring
    apart = (lax.axis_index(("pair", "core")) // block - lax.axis_index(COL) // block) % ring
    first, second = [], []
    for i in range(n):
        for j in range(n):
            if (i // block - j // block) % ring == ring // 2:
                i_way, j_way = (i + 1 * block) % n, (j + 1 * block) % n
                first.append((i * n + j, i_way * n + j_way))
                second.append((i_way * n + j_way, j * n + i))
            else:
                second.append((i * n + j, j * n + i))
    turned = lax.ppermute(outgoing[mid:], ALL, first)
    turned = lax.ppermute(jnp.where(apart == ring // 2, turned, outgoing[mid:]), ALL, second)
    local = swap(mul(far, col_x, 1, 1)) + mul(own, col_x, 1, 1)
    residual = jnp.concatenate([direct, turned], axis=0) + local
    new_amp = -residual / (row_energy.T + col_energy)
    dens = mul(far, swap(new_amp), 0, 0) + mul(own, new_amp, 0, 0)
    density = lax.ppermute(sum_over_pairs(dens), ALL, home_pairs).T
    return (new_amp, density)


def solution(mesh):
    shape = mesh.devices.shape
    grid = Mesh(mesh.devices.reshape(shape[0] // CORES, CORES, RING, shape[1] // RING), ALL)
    rows = ("pair", "core")
    placed = (
        P(rows, COL),
        P(ALL, None),
        P(ALL),
        P(ALL),
        P(),
        P(),
    )
    return jax.shard_map(
        per_device,
        mesh=grid,
        in_specs=placed,
        out_specs=(P(rows, COL), P(rows, COL)),
        check_vma=False,
    )
```

```python
import jax
import jax.numpy as jnp
from jax import lax
from jax.sharding import Mesh, PartitionSpec as P

HIGH = lax.Precision.HIGH
COL = ("x", "deep")
ALL = ("pair", "core", *COL)
CORES = 2
RING = 4


def look_up(table, index):
    hot = index[:, None] == jnp.arange(table.shape[0], dtype=jnp.int32)[None, :]
    return jnp.sum(jnp.where(hot, table[None, :], 0.0), axis=1)


def mul(a, b, da, db):
    return lax.dot_general(
        a, b, (((da,), (db,)), ((), ())), precision=HIGH, preferred_element_type=jnp.float32
    )


def per_device(amplitudes, factors, occ_map, vir_map, occ_energy, vir_energy):
    pairs, n = lax.axis_size("pair"), lax.axis_size(COL)
    core = lax.axis_index("core")
    rows, naux = factors.shape
    half = naux // CORES
    ring = lax.axis_size("x")
    flip_pairs = [(i * n + j, j * n + i) for i in range(n) for j in range(n)]
    swap_pairs = [(0, 1), (1, 0)]
    home_pairs = [
        ((p * CORES + c) * n + j, j * n + c * pairs + p)
        for p in range(pairs)
        for c in range(CORES)
        for j in range(n)
    ]

    def flip(x):
        return lax.ppermute(x, ALL, flip_pairs)

    def swap(x):
        return lax.ppermute(x, "core", swap_pairs)

    def both(own, other, axis):
        first = jnp.where(core == 0, own, other)
        second = jnp.where(core == 0, other, own)
        return jnp.stack([first, second], axis=axis)

    def split_factors(x):
        own = lax.dynamic_slice_in_dim(x, core * half, half, axis=1)
        away = lax.dynamic_slice_in_dim(x, (1 - core) * half, half, axis=1)
        return both(own, swap(away), 0).reshape(CORES * x.shape[0], half)

    def spread(x, axis, copies):
        x = jnp.broadcast_to(x[None], (copies, *x.shape))
        x = x.reshape(copies * x.shape[1], x.shape[2])
        return lax.all_to_all(x, axis, 0, 0, tiled=True)

    def sum_over_pairs(x):
        parts = lax.all_to_all(x, "pair", 0, 0, tiled=True)
        return jnp.sum(parts.reshape(pairs, x.shape[0] // pairs, x.shape[1]), axis=0)

    def shift(x, by):
        return lax.ppermute(x, "x", [(k, (k + by) % ring) for k in range(ring)])

    def ring_gather(x):
        left, right = shift(x, 1), shift(x, -1)
        part = x.shape[0] // 2
        across = [shift(right[:part], -1), shift(left[part:], 1)]
        at = lax.axis_index("x")
        out = jnp.zeros((ring, *x.shape), x.dtype)
        for by, row, block in (
            (0, 0, x), (3, 0, left), (1, 0, right), (2, 0, across[0]), (2, part, across[1])
        ):
            where = (lax.rem(at + by, ring), row, 0)
            out = lax.dynamic_update_slice(out, block[None], where)
        return out.reshape(ring * x.shape[0], x.shape[1])

    near = lax.all_gather(split_factors(factors), "deep", axis=0, tiled=True)
    row_factor = ring_gather(near)
    energy = look_up(vir_energy, vir_map) - look_up(occ_energy, occ_map)
    energy = flip(jnp.broadcast_to(jnp.pad(energy, (0, 128 - rows))[None], (8, 128)))[:, :rows]

    tile = amplitudes.shape[0]
    width = amplitudes.shape[1]
    own_amp = amplitudes.reshape(n, rows, width)
    far_amp = swap(amplitudes).reshape(n, rows, width)
    diagonal = (lax.axis_index(COL) - CORES * lax.axis_index("pair")) == jnp.arange(CORES)
    half_unit = 0.5 * jnp.eye(tile, width, dtype=jnp.float32).reshape(n, 1, rows, width)
    amp = both(own_amp, far_amp, 1) + jnp.where(diagonal[None, :, None, None], half_unit, 0.0)
    amp = amp.reshape(CORES * tile, width)

    shard = sum_over_pairs(mul(amp, row_factor, 0, 0))
    energy = jnp.pad(both(energy, swap(energy), 1)[0].reshape(CORES * rows), (0, half - CORES * rows))
    payload = jnp.concatenate([shard, jnp.broadcast_to(energy[None], (8, half))], axis=0)
    payload = spread(payload, "pair", pairs).reshape(pairs, CORES * rows + 8, half)
    col_x = payload[:, : CORES * rows].reshape(width, half)
    col_energy = payload[:, CORES * rows, : CORES * rows].reshape(1, width)
    row_energy = flip(jnp.broadcast_to(col_energy, (8, width)))[:1]
    by_core = row_factor.reshape(n, CORES, rows, half)
    own, far = [
        lax.dynamic_index_in_dim(by_core, c, 1, keepdims=False).reshape(tile, half)
        for c in (core, 1 - core)
    ]

    away = swap(mul(col_x, far, 1, 1))
    outgoing = away + lax.optimization_barrier(mul(col_x, own, 1, 1))
    local = swap(mul(far, col_x, 1, 1)) + mul(own, col_x, 1, 1)
    residual = flip(outgoing) + local
    new_amp = -residual / (row_energy.T + col_energy)
    dens = mul(far, swap(new_amp), 0, 0) + mul(own, new_amp, 0, 0)
    density = lax.ppermute(sum_over_pairs(dens), ALL, home_pairs).T
    return (new_amp, density)


def solution(mesh):
    shape = mesh.devices.shape
    grid = Mesh(mesh.devices.reshape(shape[0] // CORES, CORES, RING, shape[1] // RING), ALL)
    rows = ("pair", "core")
    placed = (
        P(rows, COL),
        P(ALL, None),
        P(ALL),
        P(ALL),
        P(),
        P(),
    )
    return jax.shard_map(
        per_device,
        mesh=grid,
        in_specs=placed,
        out_specs=(P(rows, COL), P(rows, COL)),
        check_vma=False,
    )
```

```python
import jax
import jax.numpy as jnp
from jax import lax
from jax.sharding import Mesh, PartitionSpec as P

HIGH = lax.Precision.HIGH
COL = ("x", "deep")
ALL = ("pair", "core", *COL)
CORES = 2
RING = 4


def look_up(table, index):
    hot = index[:, None] == jnp.arange(table.shape[0], dtype=jnp.int32)[None, :]
    return jnp.sum(jnp.where(hot, table[None, :], 0.0), axis=1)


def mul(a, b, da, db):
    return lax.dot_general(
        a, b, (((da,), (db,)), ((), ())), precision=HIGH, preferred_element_type=jnp.float32
    )


def per_device(amplitudes, factors, occ_map, vir_map, occ_energy, vir_energy):
    pairs, n = lax.axis_size("pair"), lax.axis_size(COL)
    core = lax.axis_index("core")
    rows, naux = factors.shape
    half = naux // CORES
    ring = lax.axis_size("x")
    flip_pairs = [(i * n + j, j * n + i) for i in range(n) for j in range(n)]
    swap_pairs = [(0, 1), (1, 0)]
    home_pairs = [
        ((p * CORES + c) * n + j, j * n + c * pairs + p)
        for p in range(pairs)
        for c in range(CORES)
        for j in range(n)
    ]

    def flip(x):
        return lax.ppermute(x, ALL, flip_pairs)

    def swap(x):
        return lax.ppermute(x, "core", swap_pairs)

    def both(own, other, axis):
        first = jnp.where(core == 0, own, other)
        second = jnp.where(core == 0, other, own)
        return jnp.stack([first, second], axis=axis)

    def split_factors(x):
        own = lax.dynamic_slice_in_dim(x, core * half, half, axis=1)
        away = lax.dynamic_slice_in_dim(x, (1 - core) * half, half, axis=1)
        return both(own, swap(away), 0).reshape(CORES * x.shape[0], half)

    def spread(x, axis, copies):
        x = jnp.broadcast_to(x[None], (copies, *x.shape))
        x = x.reshape(copies * x.shape[1], x.shape[2])
        return lax.all_to_all(x, axis, 0, 0, tiled=True)

    def sum_over_pairs(x):
        parts = lax.all_to_all(x, "pair", 0, 0, tiled=True)
        return jnp.sum(parts.reshape(pairs, x.shape[0] // pairs, x.shape[1]), axis=0)

    def shift(x, by):
        return lax.ppermute(x, "x", [(k, (k + by) % ring) for k in range(ring)])

    def ring_gather(x):
        left, right = shift(x, 1), shift(x, -1)
        part = x.shape[0] // 2
        across = [shift(right[:part], -1), shift(left[part:], 1)]
        at = lax.axis_index("x")
        out = jnp.zeros((ring, *x.shape), x.dtype)
        for by, row, block in (
            (0, 0, x), (3, 0, left), (1, 0, right), (2, 0, across[0]), (2, part, across[1])
        ):
            where = (lax.rem(at + by, ring), row, 0)
            out = lax.dynamic_update_slice(out, block[None], where)
        return out.reshape(ring * x.shape[0], x.shape[1])

    piece, far_amp = lax.optimization_barrier((split_factors(factors), swap(amplitudes)))
    near = lax.all_gather(piece, "deep", axis=0, tiled=True)
    row_factor = ring_gather(near)
    energy = look_up(vir_energy, vir_map) - look_up(occ_energy, occ_map)
    energy = jnp.broadcast_to(jnp.pad(energy, (0, 128 - rows))[None], (8, 128))
    energy, _ = lax.optimization_barrier((energy, near))
    row_energy = spread(energy, COL, n).reshape(n, 8, 128)[:, 0, :rows].reshape(1, n * rows)

    tile = amplitudes.shape[0]
    width = amplitudes.shape[1]
    own_amp = amplitudes.reshape(n, rows, width)
    far_amp = far_amp.reshape(n, rows, width)
    diagonal = (lax.axis_index(COL) - CORES * lax.axis_index("pair")) == jnp.arange(CORES)
    half_unit = 0.5 * jnp.eye(tile, width, dtype=jnp.float32).reshape(n, 1, rows, width)
    amp = both(own_amp, far_amp, 1) + jnp.where(diagonal[None, :, None, None], half_unit, 0.0)
    amp = amp.reshape(CORES * tile, width)

    amp, row_energy = lax.optimization_barrier((amp, row_energy))

    col_x = spread(sum_over_pairs(mul(amp, row_factor, 0, 0)), "pair", pairs)
    by_core = row_factor.reshape(n, CORES, rows, half)
    own, far = [
        lax.dynamic_index_in_dim(by_core, c, 1, keepdims=False).reshape(tile, half)
        for c in (core, 1 - core)
    ]

    away = swap(mul(col_x, far, 1, 1))
    outgoing = away + lax.optimization_barrier(mul(col_x, own, 1, 1))
    arrived = flip(outgoing)
    local = swap(mul(far, col_x, 1, 1)) + mul(own, col_x, 1, 1)
    row_energy, local = lax.optimization_barrier((row_energy, local))
    col_energy = flip(jnp.broadcast_to(row_energy, (8, width)))[:1]
    new_amp = -(arrived + local) / (row_energy.T + col_energy)
    dens = mul(far, swap(new_amp), 0, 0) + mul(own, new_amp, 0, 0)
    density = lax.ppermute(sum_over_pairs(dens), ALL, home_pairs).T
    return (new_amp, density)


def solution(mesh):
    shape = mesh.devices.shape
    grid = Mesh(mesh.devices.reshape(shape[0] // CORES, CORES, RING, shape[1] // RING), ALL)
    rows = ("pair", "core")
    placed = (
        P(rows, COL),
        P(ALL, None),
        P(ALL),
        P(ALL),
        P(),
        P(),
    )
    return jax.shard_map(
        per_device,
        mesh=grid,
        in_specs=placed,
        out_specs=(P(rows, COL), P(rows, COL)),
        check_vma=False,
    )
```

```python
import jax
import jax.numpy as jnp
from jax import lax
from jax.sharding import Mesh, PartitionSpec as P

HIGH = lax.Precision.HIGH
COL = ("x", "deep")
ALL = ("pair", "core", *COL)
CORES = 2
RING = 4


def look_up(table, index):
    hot = index[:, None] == jnp.arange(table.shape[0], dtype=jnp.int32)[None, :]
    return jnp.sum(jnp.where(hot, table[None, :], 0.0), axis=1)


def mul(a, b, da, db):
    return lax.dot_general(
        a, b, (((da,), (db,)), ((), ())), precision=HIGH, preferred_element_type=jnp.float32
    )


def per_device(amplitudes, factors, occ_map, vir_map, occ_energy, vir_energy):
    pairs, n = lax.axis_size("pair"), lax.axis_size(COL)
    core = lax.axis_index("core")
    rows, naux = factors.shape
    half = naux // CORES
    ring = lax.axis_size("x")
    flip_pairs = [(i * n + j, j * n + i) for i in range(n) for j in range(n)]
    swap_pairs = [(0, 1), (1, 0)]
    home_pairs = [
        ((p * CORES + c) * n + j, j * n + c * pairs + p)
        for p in range(pairs)
        for c in range(CORES)
        for j in range(n)
    ]

    def flip(x):
        return lax.ppermute(x, ALL, flip_pairs)

    def swap(x):
        return lax.ppermute(x, "core", swap_pairs)

    def both(own, other, axis):
        first = jnp.where(core == 0, own, other)
        second = jnp.where(core == 0, other, own)
        return jnp.stack([first, second], axis=axis)

    def split_factors(x):
        own = lax.dynamic_slice_in_dim(x, core * half, half, axis=1)
        away = lax.dynamic_slice_in_dim(x, (1 - core) * half, half, axis=1)
        return both(own, swap(away), 0).reshape(CORES * x.shape[0], half)

    def spread(x, axis, copies):
        x = jnp.broadcast_to(x[None], (copies, *x.shape))
        x = x.reshape(copies * x.shape[1], x.shape[2])
        return lax.all_to_all(x, axis, 0, 0, tiled=True)

    def sum_over_pairs(x):
        parts = lax.all_to_all(x, "pair", 0, 0, tiled=True)
        return jnp.sum(parts.reshape(pairs, x.shape[0] // pairs, x.shape[1]), axis=0)

    def shift(x, by):
        return lax.ppermute(x, "x", [(k, (k + by) % ring) for k in range(ring)])

    def ring_gather(x):
        left, right = shift(x, 1), shift(x, -1)
        part = x.shape[0] // 2
        across = [shift(right[:part], -1), shift(left[part:], 1)]
        at = lax.axis_index("x")
        out = jnp.zeros((ring, *x.shape), x.dtype)
        for by, row, block in (
            (0, 0, x), (3, 0, left), (1, 0, right), (2, 0, across[0]), (2, part, across[1])
        ):
            where = (lax.rem(at + by, ring), row, 0)
            out = lax.dynamic_update_slice(out, block[None], where)
        return out.reshape(ring * x.shape[0], x.shape[1]), left, right

    piece, far_amp = lax.optimization_barrier((split_factors(factors), swap(amplitudes)))
    near = lax.all_gather(piece, "deep", axis=0, tiled=True)
    row_factor, left, right = ring_gather(near)
    energy = look_up(vir_energy, vir_map) - look_up(occ_energy, occ_map)
    energy = jnp.broadcast_to(jnp.pad(energy, (0, 128 - rows))[None], (8, 128))
    energy, _ = lax.optimization_barrier((energy, near))
    row_energy = spread(energy, COL, n).reshape(n, 8, 128)[:, 0, :rows].reshape(1, n * rows)

    tile = amplitudes.shape[0]
    width = amplitudes.shape[1]
    own_amp = amplitudes.reshape(n, rows, width)
    far_amp = far_amp.reshape(n, rows, width)
    diagonal = (lax.axis_index(COL) - CORES * lax.axis_index("pair")) == jnp.arange(CORES)
    half_unit = 0.5 * jnp.eye(tile, width, dtype=jnp.float32).reshape(n, 1, rows, width)
    amp = both(own_amp, far_amp, 1) + jnp.where(diagonal[None, :, None, None], half_unit, 0.0)
    amp = amp.reshape(CORES * tile, width)

    amp, row_energy, _, _ = lax.optimization_barrier((amp, row_energy, left, right))

    col_x = spread(sum_over_pairs(mul(amp, row_factor, 0, 0)), "pair", pairs)
    by_core = row_factor.reshape(n, CORES, rows, half)
    own, far = [
        lax.dynamic_index_in_dim(by_core, c, 1, keepdims=False).reshape(tile, half)
        for c in (core, 1 - core)
    ]

    away = swap(mul(col_x, far, 1, 1))
    outgoing = away + lax.optimization_barrier(mul(col_x, own, 1, 1))
    arrived = flip(outgoing)
    local = swap(mul(far, col_x, 1, 1)) + mul(own, col_x, 1, 1)
    row_energy, local = lax.optimization_barrier((row_energy, local))
    col_energy = flip(jnp.broadcast_to(row_energy, (8, width)))[:1]
    new_amp = -(arrived + local) / (row_energy.T + col_energy)
    dens = mul(far, swap(new_amp), 0, 0) + mul(own, new_amp, 0, 0)
    density = lax.ppermute(sum_over_pairs(dens), ALL, home_pairs).T
    return (new_amp, density)


def solution(mesh):
    shape = mesh.devices.shape
    grid = Mesh(mesh.devices.reshape(shape[0] // CORES, CORES, RING, shape[1] // RING), ALL)
    rows = ("pair", "core")
    placed = (
        P(rows, COL),
        P(ALL, None),
        P(ALL),
        P(ALL),
        P(),
        P(),
    )
    return jax.shard_map(
        per_device,
        mesh=grid,
        in_specs=placed,
        out_specs=(P(rows, COL), P(rows, COL)),
        check_vma=False,
    )
```

```python
import jax
import jax.numpy as jnp
from jax import lax
from jax.sharding import Mesh, PartitionSpec as P

HIGH = lax.Precision.HIGH
COL = ("x", "deep")
ALL = ("pair", "core", *COL)
CORES = 2
RING = 4


def look_up(table, index):
    hot = index[:, None] == jnp.arange(table.shape[0], dtype=jnp.int32)[None, :]
    return jnp.sum(jnp.where(hot, table[None, :], 0.0), axis=1)


def mul(a, b, da, db):
    return lax.dot_general(
        a, b, (((da,), (db,)), ((), ())), precision=HIGH, preferred_element_type=jnp.float32
    )


def per_device(amplitudes, factors, occ_map, vir_map, occ_energy, vir_energy):
    pairs, n = lax.axis_size("pair"), lax.axis_size(COL)
    core = lax.axis_index("core")
    rows, naux = factors.shape
    half = naux // CORES
    ring = lax.axis_size("x")
    flip_pairs = [(i * n + j, j * n + i) for i in range(n) for j in range(n)]
    swap_pairs = [(0, 1), (1, 0)]
    home_pairs = [
        ((p * CORES + c) * n + j, j * n + c * pairs + p)
        for p in range(pairs)
        for c in range(CORES)
        for j in range(n)
    ]

    def flip(x):
        return lax.ppermute(x, ALL, flip_pairs)

    def swap(x):
        return lax.ppermute(x, "core", swap_pairs)

    def both(own, other, axis):
        first = jnp.where(core == 0, own, other)
        second = jnp.where(core == 0, other, own)
        return jnp.stack([first, second], axis=axis)

    def split_factors(x):
        own = lax.dynamic_slice_in_dim(x, core * half, half, axis=1)
        away = lax.dynamic_slice_in_dim(x, (1 - core) * half, half, axis=1)
        return both(own, swap(away), 0).reshape(CORES * x.shape[0], half)

    def spread(x, axis, copies):
        x = jnp.broadcast_to(x[None], (copies, *x.shape))
        x = x.reshape(copies * x.shape[1], x.shape[2])
        return lax.all_to_all(x, axis, 0, 0, tiled=True)

    def sum_over_pairs(x):
        parts = lax.all_to_all(x, "pair", 0, 0, tiled=True)
        return jnp.sum(parts.reshape(pairs, x.shape[0] // pairs, x.shape[1]), axis=0)

    def shift(x, by):
        return lax.ppermute(x, "x", [(k, (k + by) % ring) for k in range(ring)])

    def ring_gather(x):
        left, right = shift(x, 1), shift(x, -1)
        part = x.shape[0] // 2
        across = [shift(right[:part], -1), shift(left[part:], 1)]
        at = lax.axis_index("x")
        out = jnp.zeros((ring, *x.shape), x.dtype)
        for by, row, block in (
            (0, 0, x), (3, 0, left), (1, 0, right), (2, 0, across[0]), (2, part, across[1])
        ):
            where = (lax.rem(at + by, ring), row, 0)
            out = lax.dynamic_update_slice(out, block[None], where)
        return out.reshape(ring * x.shape[0], x.shape[1]), left, right

    piece, far_amp = lax.optimization_barrier((split_factors(factors), swap(amplitudes)))
    near = lax.all_gather(piece, "deep", axis=0, tiled=True)
    row_factor, left, right = ring_gather(near)
    energy = look_up(vir_energy, vir_map) - look_up(occ_energy, occ_map)
    energy = jnp.broadcast_to(jnp.pad(energy, (0, 128 - rows))[None], (8, 128))
    energy, _ = lax.optimization_barrier((energy, near))
    row_energy = spread(energy, COL, n).reshape(n, 8, 128)[:, 0, :rows].reshape(1, n * rows)

    tile = amplitudes.shape[0]
    width = amplitudes.shape[1]
    own_amp = amplitudes.reshape(n, rows, width)
    far_amp = far_amp.reshape(n, rows, width)
    amp = both(own_amp, far_amp, 1)
    place = [lax.broadcasted_iota(jnp.int32, amp.shape, k) for k in range(4)]
    mine = place[1] == lax.axis_index(COL) - CORES * lax.axis_index("pair")
    diagonal = mine & (place[0] * rows + place[2] == place[3])
    amp = amp + jnp.where(diagonal, 0.5, 0.0)
    amp = amp.reshape(CORES * tile, width)

    amp, row_energy, _, _ = lax.optimization_barrier((amp, row_energy, left, right))

    col_x = spread(sum_over_pairs(mul(amp, row_factor, 0, 0)), "pair", pairs)
    by_core = row_factor.reshape(n, CORES, rows, half)
    own, far = [
        lax.dynamic_index_in_dim(by_core, c, 1, keepdims=False).reshape(tile, half)
        for c in (core, 1 - core)
    ]

    away = swap(mul(col_x, far, 1, 1))
    outgoing = away + lax.optimization_barrier(mul(col_x, own, 1, 1))
    arrived = flip(outgoing)
    local = swap(mul(far, col_x, 1, 1)) + mul(own, col_x, 1, 1)
    row_energy, local = lax.optimization_barrier((row_energy, local))
    col_energy = flip(jnp.broadcast_to(row_energy, (8, width)))[:1]
    new_amp = -(arrived + local) / (row_energy.T + col_energy)
    dens = mul(far, swap(new_amp), 0, 0) + mul(own, new_amp, 0, 0)
    density = lax.ppermute(sum_over_pairs(dens), ALL, home_pairs).T
    return (new_amp, density)


def solution(mesh):
    shape = mesh.devices.shape
    grid = Mesh(mesh.devices.reshape(shape[0] // CORES, CORES, RING, shape[1] // RING), ALL)
    rows = ("pair", "core")
    placed = (
        P(rows, COL),
        P(ALL, None),
        P(ALL),
        P(ALL),
        P(),
        P(),
    )
    return jax.shard_map(
        per_device,
        mesh=grid,
        in_specs=placed,
        out_specs=(P(rows, COL), P(rows, COL)),
        check_vma=False,
    )
```
